32 devices in a mesh: rows: 16 (over z, y, x), cols: 2 (over core).
Axes of the slice: x: 2, y: 2, z: 4, core: 2. Of those that a mesh axis runs over, the one named last changes fastest.
Arguments:
- node_feat: bfloat16 [16, 2, 128, 256], P('rows', 'cols'), may hold values from -6 to 6
- species: int32 [16, 2, 128], P('rows', 'cols'), may hold values from 0 to 1
- layer_embed: bfloat16 [2, 256], replicated, may hold values from -6 to 6
- w_src: bfloat16 [256, 128], replicated, may hold values from -0.375 to 0.375
- w_dst: bfloat16 [256, 128], replicated, may hold values from -0.375 to 0.375
- w_rad: float32 [16, 128], replicated, may hold values from -3 to 3
- w_mid: bfloat16 [128, 128], replicated, may hold values from -0.5 to 0.5
- w_out: bfloat16 [128, 169], replicated, may hold values from -0.5 to 0.5
- w_self: bfloat16 [256, 169], replicated, may hold values from -0.375 to 0.375
- bond_target: int32 [16, 2, 24, 128], P('rows', 'cols'), may hold values from 0 to 1151, as said below
- bond_live: int32 [16, 2, 24, 128], P('rows', 'cols'), may hold values from 0 to 1
- bond_len: float32 [16, 2, 24, 128], P('rows', 'cols'), may hold values from 1.4 to 6
- probes: float32 [16, 2, 128, 208], P('rows', 'cols'), may hold values from -6 to 6
- cheb_coef: float32 [5], replicated, may hold values from -1 to 1
Outputs:
- fermi_probes: float32 [16, 2, 128, 208], P('rows', 'cols')
The draws below stay inside these ranges and needn't reach their ends.
Inputs may be any that keep to these rules, and one draw needn't show every extreme that they name: bond_target = b * 128 + j names atom j of the block at offset (b // 3 - 1, b % 3 - 1) in (long, short) direction from the bond's own block.
All inputs are finite; a program needn't handle non-finite values.
Results may differ from the reference program's by a relative error of at most 0.008.
Values may be sent and summed in bfloat16 or wider, within the bound.
A program may use at most 128 MiB of HBM per device.

```python
import jax
import jax.numpy as jnp
from jax import lax

ATOMS = 128
SLOTS = 24
FEATURES = 256
CHANNELS = 128
RADIAL = 16
ORBITALS = 13
PROBES = 16
STEPS = 4
GRID_R = 16
GRID_C = 2


def draw_bond_target(key, part):
    key = jax.random.fold_in(key, 11)
    key_pick, key_other, key_atom = jax.random.split(key, 3)
    grid_shape = (GRID_R, GRID_C, SLOTS, ATOMS)
    pick_own = jax.random.randint(key_pick, grid_shape, 0, 10)
    other_code = jax.random.randint(key_other, grid_shape, 0, 8)
    block_code = jnp.where(pick_own < 6, 4, other_code + (other_code >= 4).astype(jnp.int32))
    atom_pick = jax.random.randint(key_atom, grid_shape, 0, ATOMS)
    target = (block_code * ATOMS + atom_pick).astype(jnp.int32)
    target = target.at[0, 0, 0, 0].set(0)
    target = target.at[0, 0, 0, 1].set(9 * ATOMS - 1)
    return target


def draw_bond_live(key, part):
    key = jax.random.fold_in(key, 23)
    key_base, key_roll = jax.random.split(key, 2)
    grid_shape = (GRID_R, GRID_C, SLOTS, ATOMS)
    row_ids = jnp.arange(GRID_R).astype(jnp.int32)[:, None, None, None]
    live_limit = 35 + 60 * row_ids // max(GRID_R - 1, 1)
    device_base = jax.random.randint(key_base, (GRID_R, GRID_C, 1, 1), 0, 10)
    roll_draw = jax.random.randint(key_roll, grid_shape, 0, 100)
    return (roll_draw < live_limit + device_base).astype(jnp.int32)


def touch_ends(values, own_key, low, high):
    place = [jax.random.randint(jax.random.fold_in(own_key, axis), (), 0, length) for axis, length in enumerate(values.shape)]
    main_axis = values.shape.index(max(values.shape))
    next_to = place[:main_axis] + [(place[main_axis] + 1) % values.shape[main_axis]] + place[main_axis + 1:]
    return values.at[tuple(place)].set(low).at[tuple(next_to)].set(high)


def block_scale(key, dims, cuts, low, high):
    def one(axis_at, blocks):
        draws = jax.random.uniform(jax.random.fold_in(jax.random.fold_in(key, 6), axis_at), (blocks,), jnp.float32, low / len(cuts), high / len(cuts))
        return jnp.repeat(jnp.exp(draws), dims[axis_at] // blocks).reshape((-1,) + (1,) * (len(dims) - axis_at - 1))

    level = one(*cuts[0])
    for cut in cuts[1:]:
        level = level * one(*cut)
    return level


def scatter_about(stream_key, extent, deviation, limit, cuts=(), held_as=jnp.bfloat16):
    array = deviation * jax.random.normal(stream_key, extent, jnp.float32)
    if cuts:
        array = array * block_scale(stream_key, extent, cuts, -0.22, 0.18)
    return jnp.clip(array, -limit, limit).astype(held_as)


def setup_inputs(seed: int = 0) -> dict:
    seeds = jax.random.split(jax.random.key(seed), 15)
    node_feat = scatter_about(seeds[0], (GRID_R, GRID_C, ATOMS, FEATURES), 1.0, 6.0, ((0, 16), (1, 2)))
    species = touch_ends(jax.random.randint(seeds[1], (GRID_R, GRID_C, ATOMS), 0, 2), jax.random.fold_in(seeds[1], 1), 0, 1).astype(jnp.int32)
    layer_embed = scatter_about(seeds[2], (2, FEATURES), 1.0, 6.0)
    w_src = scatter_about(seeds[3], (FEATURES, CHANNELS), FEATURES ** -0.5, 0.375)
    w_dst = scatter_about(seeds[4], (FEATURES, CHANNELS), FEATURES ** -0.5, 0.375)
    w_rad = scatter_about(seeds[5], (RADIAL, CHANNELS), 4 ** -0.5, 3.0, (), jnp.float32)
    w_mid = scatter_about(seeds[6], (CHANNELS, CHANNELS), CHANNELS ** -0.5, 0.5)
    w_out = scatter_about(seeds[7], (CHANNELS, ORBITALS * ORBITALS), CHANNELS ** -0.5, 0.5)
    w_self = scatter_about(seeds[8], (FEATURES, ORBITALS * ORBITALS), FEATURES ** -0.5, 0.375)
    bond_target = draw_bond_target(jax.random.fold_in(seeds[14], 71), 0)
    bond_live = draw_bond_live(jax.random.fold_in(seeds[14], 71), 0)
    bond_len = jnp.clip(1.4 + 4.6 * jax.random.uniform(seeds[11], (GRID_R, GRID_C, SLOTS, ATOMS), jnp.float32) ** block_scale(seeds[11], (GRID_R, GRID_C, SLOTS, ATOMS), ((0, 16), (1, 2)), -0.2, 0.2), 1.4, 6.0)
    probes = scatter_about(seeds[12], (GRID_R, GRID_C, ATOMS, ORBITALS * PROBES), 1.0, 6.0, ((0, 16), (1, 2)), jnp.float32)
    cheb_coef = jnp.clip(jax.random.uniform(seeds[13], (STEPS + 1,), jnp.float32, -1.0, 1.0), -1.0, 1.0)
    return {"node_feat": node_feat, "species": species, "layer_embed": layer_embed, "w_src": w_src, "w_dst": w_dst, "w_rad": w_rad, "w_mid": w_mid, "w_out": w_out, "w_self": w_self, "bond_target": bond_target, "bond_live": bond_live, "bond_len": bond_len, "probes": probes, "cheb_coef": cheb_coef}


stretch_factor = 6.0
basis_sharpness = 1.5


def radial(length):
    centers = 1.0 + 5.0 * jnp.arange(RADIAL).astype(jnp.float32) / (RADIAL - 1)
    return jnp.exp(-basis_sharpness * (length[..., None] - centers) ** 2)


def reference(node_feat, species, layer_embed, w_src, w_dst, w_rad, w_mid, w_out, w_self, bond_target, bond_live, bond_len, probes, cheb_coef):
    grid_r = node_feat.shape[0]
    grid_c = node_feat.shape[1]
    layer_row = jnp.where(species[..., None] == 0, layer_embed[0].astype(jnp.float32), layer_embed[1].astype(jnp.float32))
    mixed_feat = (node_feat.astype(jnp.float32) + layer_row).astype(jnp.bfloat16)
    flat_mixed = mixed_feat.reshape(-1, FEATURES)
    source = jnp.dot(flat_mixed, w_src, preferred_element_type=jnp.float32).astype(jnp.bfloat16).reshape(grid_r, grid_c, ATOMS, CHANNELS)
    target = jnp.dot(flat_mixed, w_dst, preferred_element_type=jnp.float32).astype(jnp.bfloat16).reshape(grid_r, grid_c, ATOMS, CHANNELS)
    self_raw = jnp.dot(flat_mixed, w_self, preferred_element_type=jnp.float32).reshape(-1, ATOMS, ORBITALS, ORBITALS)
    onsite = (0.5 * (self_raw + jnp.swapaxes(self_raw, -1, -2))).astype(jnp.bfloat16)
    padded = jnp.pad(target, ((1, 1), (1, 1), (0, 0), (0, 0)))
    devices = jnp.arange(grid_r * grid_c).astype(jnp.int32)

    def bond_blocks(device):
        row_id = device // grid_c
        col_id = device % grid_c
        zero = jnp.zeros((), jnp.int32)
        window = lax.dynamic_slice(padded, (row_id, col_id, zero, zero), (3, 3, ATOMS, CHANNELS)).reshape(9 * ATOMS, CHANNELS)
        slot_index = bond_target[row_id, col_id].reshape(-1)
        far_rows = jnp.take(window, slot_index, axis=0).reshape(SLOTS, ATOMS, CHANNELS)
        lifted = jnp.einsum("kar,rc->kac", radial(bond_len[row_id, col_id]), w_rad, precision=lax.Precision.HIGHEST)
        edge_act = jax.nn.silu(source[row_id, col_id].astype(jnp.float32)[None] + far_rows.astype(jnp.float32) + lifted).astype(jnp.bfloat16)
        hidden_act = jax.nn.silu(jnp.dot(edge_act.reshape(-1, CHANNELS), w_mid, preferred_element_type=jnp.float32)).astype(jnp.bfloat16)
        bond_block = jnp.dot(hidden_act, w_out, preferred_element_type=jnp.float32) * bond_live[row_id, col_id].reshape(-1, 1).astype(jnp.float32)
        return bond_block.astype(jnp.bfloat16).reshape(SLOTS, ATOMS, ORBITALS, ORBITALS)

    blocks = lax.map(bond_blocks, devices)
    row_sums = jnp.sum(jnp.abs(onsite.astype(jnp.float32)), axis=-1) + jnp.sum(jnp.abs(blocks.astype(jnp.float32)), axis=(1, 4))
    radius = jnp.max(row_sums)
    vec_width = ORBITALS * PROBES

    def apply_scaled(vector):
        padded_vec = jnp.pad(vector, ((1, 1), (1, 1), (0, 0), (0, 0)))

        def per_device(device):
            row_id = device // grid_c
            col_id = device % grid_c
            zero = jnp.zeros((), jnp.int32)
            window = lax.dynamic_slice(padded_vec, (row_id, col_id, zero, zero), (3, 3, ATOMS, vec_width)).reshape(9 * ATOMS, vec_width)
            neighbor_vec = jnp.take(window, bond_target[row_id, col_id].reshape(-1), axis=0).reshape(SLOTS, ATOMS, ORBITALS, PROBES)
            own_part = lax.dynamic_slice(vector, (row_id, col_id, zero, zero), (1, 1, ATOMS, vec_width)).reshape(ATOMS, ORBITALS, PROBES)
            summed = jnp.einsum("kaij,kajp->aip", blocks[device].astype(jnp.float32), neighbor_vec, precision=lax.Precision.HIGHEST)
            summed = summed + jnp.einsum("aij,ajp->aip", onsite[device].astype(jnp.float32), own_part, precision=lax.Precision.HIGHEST)
            return summed.reshape(ATOMS, vec_width)

        return (stretch_factor / radius) * lax.map(per_device, devices).reshape(grid_r, grid_c, ATOMS, vec_width)

    previous = probes
    current = apply_scaled(probes)
    summed_all = cheb_coef[0] * previous + cheb_coef[1] * current
    for order in range(2, STEPS + 1):
        following = 2.0 * apply_scaled(current) - previous
        summed_all = summed_all + cheb_coef[order] * following
        previous = current
        current = following
    return summed_all
```

```python
import functools

import jax
import jax.numpy as jnp
from jax import lax
from jax.experimental import pallas as pl
from jax.experimental.pallas import tpu as pltpu
from jax.sharding import PartitionSpec as P

RADIAL = 16
ORBITALS = 13
PROBES = 16
STEPS = 4
VEC = ORBITALS * PROBES
PAIRS = ORBITALS * ORBITALS
SPAN = 176

stretch_factor = 6.0
basis_sharpness = 1.5
MESH = pl.DeviceIdType.MESH
f32 = jnp.float32
bf16 = jnp.bfloat16


def silu(x):
    return x * (0.5 * jnp.tanh(0.5 * x) + 0.5)


def dot_tn(a, b):
    return lax.dot_general(a, b, (((0,), (0,)), ((), ())), preferred_element_type=f32)


def kernel(
    n_rows,
    rounds,
    node_ref,
    species_ref,
    embed_ref,
    wsrc_ref,
    wdst_ref,
    wrad_ref,
    wmid_ref,
    wout_ref,
    wself_ref,
    tgt_ref,
    live_ref,
    len_ref,
    probes_ref,
    coef_ref,
    out_ref,
    first,
    vecs,
    onehot,
    index,
    blocks,
    source,
    split,
    keep,
    wide,
    tall,
    rad,
    far,
    send_sem,
    recv_sem,
    rsend_sem,
    rrecv_sem,
):
    atoms = node_ref.shape[0]
    slots = tgt_ref.shape[0]
    channels = wsrc_ref.shape[1]
    r = lax.axis_index("rows")
    c = lax.axis_index("cols")
    oc = 1 - c
    has_up = r > 0
    has_down = r < n_rows - 1
    ways = [
        (-1, 0, has_up),
        (-1, 1, has_up),
        (1, 0, has_down),
        (1, 1, has_down),
        (0, 1, None),
    ]

    def when(cond, fn):
        if cond is None:
            fn()
        else:
            pl.when(cond)(fn)

    def place(step, other):
        return (step + 1) * 2 + other

    def partner(q):
        if q == 0:
            return (r, oc)
        w = 1 << (q - 1)
        return (r + w - 2 * w * ((r // w) % 2), c)

    barrier = pltpu.get_barrier_semaphore()
    for step, other, cond in ways:

        def greet(step=step, other=other):
            pl.semaphore_signal(
                barrier, inc=1, device_id=(r + step, oc if other else c), device_id_type=MESH
            )

        when(cond, greet)
    for q in range(1, rounds):
        pl.semaphore_signal(barrier, inc=1, device_id=partner(q), device_id_type=MESH)

    species_col = jnp.broadcast_to(species_ref[...].astype(f32), (atoms, atoms)).T
    species_col = jnp.concatenate([species_col] * (node_ref.shape[1] // atoms), axis=1)
    embed = embed_ref[...].astype(f32)
    mixed = (
        node_ref[...].astype(f32)
        + jnp.where(species_col == 0.0, embed[0:1, :], embed[1:2, :])
    ).astype(bf16)
    target = jnp.dot(mixed, wdst_ref[...], preferred_element_type=f32)
    own = pl.ds(place(0, 0) * atoms, atoms)
    first[0:channels, own] = target.T.astype(bf16)
    wide[...] = jnp.zeros_like(wide)
    wide[:, 0:VEC] = probes_ref[...]
    start = jnp.concatenate(
        [wide[:, i * atoms : (i + 1) * atoms].T for i in range(wide.shape[1] // atoms)], axis=0
    )[0:VEC]
    keep[0] = start
    first[channels : channels + VEC, own] = start.astype(bf16)

    for cond, step in ((has_up, -1), (has_down, 1)):

        def clear(step=step):
            cols = pl.ds(place(step, 0) * atoms, 2 * atoms)
            first[:, cols] = jnp.zeros((first.shape[0], 2 * atoms), bf16)
            for n in range(STEPS - 1):
                vecs[n, :, cols] = jnp.zeros((VEC, 2 * atoms), bf16)

        pl.when(jnp.logical_not(cond))(clear)

    def buffer(n):
        return first if n == 0 else vecs.at[n - 1]

    def copy(n, w, arriving):
        buf = buffer(n)
        step, other, _ = ways[w]
        back = w if step == 0 else (w + 2) % 4
        to = place(step, other) if arriving else place(-step, other)
        return pltpu.make_async_remote_copy(
            src_ref=buf.at[:, own],
            dst_ref=buf.at[:, pl.ds(to * atoms, atoms)],
            send_sem=send_sem.at[n, w],
            recv_sem=recv_sem.at[n, w if arriving else back],
            device_id=(r + step, oc if other else c),
            device_id_type=MESH,
        )

    def send(n):
        for w, (_, _, cond) in enumerate(ways):
            when(cond, lambda w=w: copy(n, w, False).start())

    def receive(n):
        for w, (_, _, cond) in enumerate(ways):
            when(cond, lambda w=w: copy(n, w, True).wait_recv())

    def finish(n):
        for w, (_, _, cond) in enumerate(ways):
            when(cond, lambda w=w: copy(n, w, False).wait_send())

    pl.semaphore_wait(
        barrier, rounds + 2 * jnp.where(has_up, 1, 0) + 2 * jnp.where(has_down, 1, 0)
    )
    send(0)

    bt = tgt_ref[...]
    b = bt // atoms
    dr = jnp.where(b >= 3, 1, 0) + jnp.where(b >= 6, 1, 0)
    dc = b - 3 * dr - 1
    other = jnp.where(dc == oc - c, 1, 0)
    valid = (dc == 0) | (dc == oc - c)
    index[...] = jnp.where(valid, (dr * 2 + other) * atoms + (bt - b * atoms), -1)
    two = 2 * atoms

    def pair_row(ref, k):
        return jnp.concatenate([ref[pl.ds(2 * k, 1), :], ref[pl.ds(2 * k + 1, 1), :]], axis=1)

    def mark(k, carry):
        row = pair_row(index, k)
        ids = lax.broadcasted_iota(jnp.int32, (6 * atoms, two), 0)
        onehot[k] = jnp.where(ids == row, 1.0, 0.0).astype(bf16)
        return carry

    lax.fori_loop(0, slots // 2, mark, 0)

    source_t = jnp.dot(mixed, wsrc_ref[...], preferred_element_type=f32).T
    source_t = source_t.astype(bf16).astype(f32)
    source[...] = jnp.concatenate([source_t, source_t], axis=1)
    wrad = wrad_ref[...]
    w_hi = wrad.astype(bf16)
    w_lo = (wrad - w_hi.astype(f32)).astype(bf16)
    split[...] = jnp.concatenate([w_hi, w_hi, w_lo], axis=0)
    centers = 1.0 + 5.0 * lax.broadcasted_iota(jnp.int32, (RADIAL, two), 0).astype(f32) / (
        RADIAL - 1
    )
    raw = lax.dot_general(
        wself_ref[...], mixed, (((0,), (1,)), ((), ())), preferred_element_type=f32
    )
    far[0:PAIRS, 0:atoms] = raw
    for i in range(ORBITALS):
        for j in range(i, ORBITALS):
            p, q = i * ORBITALS + j, j * ORBITALS + i
            mean = 0.5 * (far[p : p + 1, 0:atoms] + far[q : q + 1, 0:atoms])
            mean = mean.astype(bf16).astype(f32)
            blocks[slots, p : p + 1, :] = mean
            if p != q:
                blocks[slots, q : q + 1, :] = mean

    def block_apply(k, parts, acc):
        acc = list(acc)
        for j in range(ORBITALS):
            n = parts(j)
            for i in range(ORBITALS):
                acc[i] = acc[i] + blocks[k, pl.ds(i * ORBITALS + j, 1), :] * n
        return tuple(acc)

    def own_apply(vec, acc):
        return block_apply(slots, lambda j: vec[j * PROBES : (j + 1) * PROBES], acc)

    def gathered(k, acc):
        for h in range(2):
            acc = block_apply(
                2 * k + h,
                lambda j: far[
                    channels + j * PROBES : channels + (j + 1) * PROBES,
                    h * atoms : (h + 1) * atoms,
                ],
                acc,
            )
        return acc

    zero = tuple(jnp.zeros((PROBES, atoms), f32) for _ in range(ORBITALS))
    receive(0)

    def bond_step(k, carry):
        acc, total = carry
        far[...] = jnp.dot(first[...], onehot[k], preferred_element_type=f32)
        length = pair_row(len_ref, k)
        basis = jnp.exp(-basis_sharpness * (length - centers) ** 2)
        b_hi = basis.astype(bf16)
        b_lo = (basis - b_hi.astype(f32)).astype(bf16)
        lifted = dot_tn(split[...], jnp.concatenate([b_hi, b_lo, b_hi], axis=0))
        edge = silu(source[...] + far[0:channels, :] + lifted).astype(bf16)
        hidden = silu(dot_tn(wmid_ref[...], edge)).astype(bf16)
        made = dot_tn(wout_ref[...], hidden) * pair_row(live_ref, k).astype(f32)
        made = made.astype(bf16).astype(f32)
        blocks[2 * k, 0:PAIRS, :] = made[:, 0:atoms]
        blocks[2 * k + 1, 0:PAIRS, :] = made[:, atoms:two]
        tall[0:PAIRS, :] += jnp.abs(made[:, 0:atoms]) + jnp.abs(made[:, atoms:two])
        return gathered(k, acc), total

    tall[0:PAIRS, :] = jnp.abs(blocks[slots, 0:PAIRS, :])
    acc, _ = lax.fori_loop(0, slots // 2, bond_step, (own_apply(keep[0], zero), 0))
    y1 = jnp.concatenate(acc, axis=0)
    vecs[0, :, own] = y1.astype(bf16)
    send(1)
    keep[1] = y1

    biggest = jnp.zeros((1, atoms), f32)
    for i in range(ORBITALS):
        row = jnp.sum(tall[i * ORBITALS : (i + 1) * ORBITALS, :], axis=0, keepdims=True)
        biggest = jnp.maximum(biggest, row)
    rad[0] = jnp.broadcast_to(biggest, rad.shape[1:])

    def radius_copy(q):
        return pltpu.make_async_remote_copy(
            src_ref=rad.at[q],
            dst_ref=rad.at[rounds + 1 + q],
            send_sem=rsend_sem.at[q],
            recv_sem=rrecv_sem.at[q],
            device_id=partner(q),
            device_id_type=MESH,
        )

    def radius_turn(q):
        radius_copy(q).wait_recv()
        rad[q + 1] = jnp.maximum(rad[q], rad[rounds + 1 + q])
        if q + 1 < rounds:
            radius_copy(q + 1).start()

    radius_copy(0).start()

    def apply_part(n, lo, hi, acc):
        def step(k, acc):
            far[pl.ds(channels, VEC), :] = jnp.dot(
                vecs[n - 1], onehot[k], preferred_element_type=f32
            )
            return gathered(k, acc)

        return lax.fori_loop(lo, hi, step, acc)

    half = slots // 2
    acc = own_apply(y1, zero)
    radius_turn(0)
    radius_turn(1)
    receive(1)
    turns = list(range(2, rounds))
    cuts = [half * i // (len(turns) + 1) for i in range(len(turns) + 2)]
    for i in range(len(turns) + 1):
        acc = apply_part(1, cuts[i], cuts[i + 1], acc)
        if i < len(turns):
            radius_turn(turns[i])
    radius = jnp.max(rad[rounds], keepdims=True)
    scale = stretch_factor / radius

    t0 = keep[0]
    t1 = scale[0:1, 0:1] * keep[1]
    t2 = 2.0 * (scale[0:1, 0:1] * (scale[0:1, 0:1] * jnp.concatenate(acc, axis=0))) - t0
    vecs[1, :, own] = t2.astype(bf16)
    send(2)
    keep[1] = t1
    keep[2] = t2
    keep[0] = coef_ref[0] * t0 + coef_ref[1] * t1 + coef_ref[2] * t2
    acc = own_apply(keep[2], zero)
    receive(2)
    acc = apply_part(2, 0, half, acc)
    t3 = 2.0 * (scale[0:1, 0:1] * jnp.concatenate(acc, axis=0)) - keep[1]
    vecs[2, :, own] = t3.astype(bf16)
    send(3)
    keep[1] = t3
    keep[0] = keep[0] + coef_ref[3] * t3
    acc = own_apply(keep[1], zero)
    receive(3)
    acc = apply_part(3, 0, half, acc)
    t4 = 2.0 * (scale[0:1, 0:1] * jnp.concatenate(acc, axis=0)) - keep[2]
    tall[0:VEC, :] = keep[0] + coef_ref[4] * t4
    tall[VEC:, :] = jnp.zeros((tall.shape[0] - VEC, atoms), f32)
    for i in range(tall.shape[0] // atoms):
        wide[:, i * atoms : (i + 1) * atoms] = tall[i * atoms : (i + 1) * atoms, :].T
    out_ref[...] = wide[:, 0:VEC]
    for n in range(STEPS):
        finish(n)
    for q in range(rounds):
        radius_copy(q).wait_send()


def body(n_rows, *args):
    (node, species, embed, wsrc, wdst, wrad, wmid, wout, wself, tgt, live, length, probes, coef) = args
    atoms = node.shape[2]
    slots = tgt.shape[2]
    channels = wsrc.shape[1]
    rounds = n_rows.bit_length()
    vmem = pl.BlockSpec(memory_space=pltpu.VMEM)
    lanes = 2 * atoms
    tall_rows = 2 * atoms
    out = pl.pallas_call(
        functools.partial(kernel, n_rows, rounds),
        out_shape=jax.ShapeDtypeStruct((atoms, VEC), f32),
        in_specs=[vmem] * 13 + [pl.BlockSpec(memory_space=pltpu.SMEM)],
        out_specs=vmem,
        scratch_shapes=[
            pltpu.VMEM((channels + VEC, 6 * atoms), bf16),
            pltpu.VMEM((STEPS - 1, VEC, 6 * atoms), bf16),
            pltpu.VMEM((slots // 2, 6 * atoms, lanes), bf16),
            pltpu.VMEM((slots, atoms), jnp.int32),
            pltpu.VMEM((slots + 1, SPAN, atoms), f32),
            pltpu.VMEM((channels, lanes), f32),
            pltpu.VMEM((3 * RADIAL, channels), bf16),
            pltpu.VMEM((3, VEC, atoms), f32),
            pltpu.VMEM((atoms, tall_rows), f32),
            pltpu.VMEM((tall_rows, atoms), f32),
            pltpu.VMEM((2 * rounds + 1, 8, atoms), f32),
            pltpu.VMEM((channels + VEC, lanes), f32),
            pltpu.SemaphoreType.DMA((STEPS, 5)),
            pltpu.SemaphoreType.DMA((STEPS, 5)),
            pltpu.SemaphoreType.DMA((rounds,)),
            pltpu.SemaphoreType.DMA((rounds,)),
        ],
        compiler_params=pltpu.CompilerParams(
            collective_id=0, has_side_effects=True, vmem_limit_bytes=40 * 1024 * 1024
        ),
    )(
        node[0, 0], species[0], embed, wsrc, wdst, wrad, wmid, wout, wself,
        tgt[0, 0], live[0, 0], length[0, 0], probes[0, 0], coef,
    )
    return out[None, None]


def solution(mesh):
    n_rows = mesh.shape["rows"]
    block4 = P("rows", "cols", None, None)
    placed = (
        block4, P("rows", "cols", None), P(), P(), P(), P(), P(), P(), P(),
        block4, block4, block4, block4, P(),
    )
    return jax.shard_map(
        functools.partial(body, n_rows), mesh=mesh, in_specs=placed, out_specs=block4, check_vma=False
    )
```

```python
import functools

import jax
import jax.numpy as jnp
from jax import lax
from jax.experimental import pallas as pl
from jax.experimental.pallas import tpu as pltpu
from jax.sharding import PartitionSpec as P

RADIAL = 16
ORBITALS = 13
PROBES = 16
STEPS = 4
VEC = ORBITALS * PROBES
PAIRS = ORBITALS * ORBITALS
SPAN = 176

stretch_factor = 6.0
basis_sharpness = 1.5
MESH = pl.DeviceIdType.MESH
f32 = jnp.float32
bf16 = jnp.bfloat16


def silu(x):
    return x * (0.5 * jnp.tanh(0.5 * x) + 0.5)


def dot_tn(a, b):
    return lax.dot_general(a, b, (((0,), (0,)), ((), ())), preferred_element_type=f32)


def kernel(
    n_rows,
    rounds,
    node_ref,
    species_ref,
    embed_ref,
    wsrc_ref,
    wdst_ref,
    wrad_ref,
    wmid_ref,
    wout_ref,
    wself_ref,
    tgt_ref,
    live_ref,
    len_ref,
    probes_ref,
    coef_ref,
    out_ref,
    first,
    vecs,
    onehot,
    index,
    blocks,
    source,
    split,
    keep,
    wide,
    tall,
    rad,
    far,
    near,
    send_sem,
    recv_sem,
    rsend_sem,
    rrecv_sem,
):
    atoms = node_ref.shape[0]
    slots = tgt_ref.shape[0]
    channels = wsrc_ref.shape[1]
    r = lax.axis_index("rows")
    c = lax.axis_index("cols")
    oc = 1 - c
    has_up = r > 0
    has_down = r < n_rows - 1
    ways = [
        (-1, 0, has_up),
        (-1, 1, has_up),
        (1, 0, has_down),
        (1, 1, has_down),
        (0, 1, None),
    ]

    def when(cond, fn):
        if cond is None:
            fn()
        else:
            pl.when(cond)(fn)

    def place(step, other):
        return (step + 1) * 2 + other

    def partner(q):
        if q == 0:
            return (r, oc)
        w = 1 << (q - 1)
        return (r + w - 2 * w * ((r // w) % 2), c)

    barrier = pltpu.get_barrier_semaphore()
    for step, other, cond in ways:

        def greet(step=step, other=other):
            pl.semaphore_signal(
                barrier, inc=1, device_id=(r + step, oc if other else c), device_id_type=MESH
            )

        when(cond, greet)
    for q in range(1, rounds):
        pl.semaphore_signal(barrier, inc=1, device_id=partner(q), device_id_type=MESH)

    species_col = jnp.broadcast_to(species_ref[...].astype(f32), (atoms, atoms)).T
    species_col = jnp.concatenate([species_col] * (node_ref.shape[1] // atoms), axis=1)
    embed = embed_ref[...].astype(f32)
    mixed = (
        node_ref[...].astype(f32)
        + jnp.where(species_col == 0.0, embed[0:1, :], embed[1:2, :])
    ).astype(bf16)
    target = jnp.dot(mixed, wdst_ref[...], preferred_element_type=f32)
    own = pl.ds(place(0, 0) * atoms, atoms)
    first[0:channels, own] = target.T.astype(bf16)
    wide[...] = jnp.zeros_like(wide)
    wide[:, 0:VEC] = probes_ref[...]
    start = jnp.concatenate(
        [wide[:, i * atoms : (i + 1) * atoms].T for i in range(wide.shape[1] // atoms)], axis=0
    )[0:VEC]
    keep[0] = start
    first[channels : channels + VEC, own] = start.astype(bf16)

    for cond, step in ((has_up, -1), (has_down, 1)):

        def clear(step=step):
            cols = pl.ds(place(step, 0) * atoms, 2 * atoms)
            first[:, cols] = jnp.zeros((first.shape[0], 2 * atoms), bf16)
            for n in range(STEPS - 1):
                vecs[n, :, cols] = jnp.zeros((VEC, 2 * atoms), bf16)

        pl.when(jnp.logical_not(cond))(clear)

    def buffer(n):
        return first if n == 0 else vecs.at[n - 1]

    def copy(n, w, arriving):
        buf = buffer(n)
        step, other, _ = ways[w]
        if step != 0 and other:
            return pltpu.make_async_remote_copy(
                src_ref=buf.at[:, pl.ds(place(step, 0) * atoms, atoms)],
                dst_ref=buf.at[:, pl.ds(place(step, 1) * atoms, atoms)],
                send_sem=send_sem.at[n, w],
                recv_sem=recv_sem.at[n, w],
                device_id=(r, oc),
                device_id_type=MESH,
            )
        back = w if step == 0 else (w + 2) % 4
        to = place(step, other) if arriving else place(-step, other)
        return pltpu.make_async_remote_copy(
            src_ref=buf.at[:, own],
            dst_ref=buf.at[:, pl.ds(to * atoms, atoms)],
            send_sem=send_sem.at[n, w],
            recv_sem=recv_sem.at[n, w if arriving else back],
            device_id=(r + step, oc if other else c),
            device_id_type=MESH,
        )

    def send(n):
        for w in (0, 2, 4):
            when(ways[w][2], lambda w=w: copy(n, w, False).start())

    def receive(n):
        for w in (0, 2):

            def forward(w=w):
                copy(n, w, True).wait_recv()
                copy(n, w + 1, False).start()

            when(ways[w][2], forward)
        for w in (4, 1, 3):
            when(ways[w][2], lambda w=w: copy(n, w, True).wait_recv())

    def finish(n):
        for w, (_, _, cond) in enumerate(ways):
            when(cond, lambda w=w: copy(n, w, False).wait_send())

    pl.semaphore_wait(
        barrier, rounds + 2 * jnp.where(has_up, 1, 0) + 2 * jnp.where(has_down, 1, 0)
    )
    send(0)

    bt = tgt_ref[...]
    b = bt // atoms
    dr = jnp.where(b >= 3, 1, 0) + jnp.where(b >= 6, 1, 0)
    dc = b - 3 * dr - 1
    other = jnp.where(dc == oc - c, 1, 0)
    valid = (dc == 0) | (dc == oc - c)
    index[...] = jnp.where(valid, (dr * 2 + other) * atoms + (bt - b * atoms), -1)
    two = 2 * atoms

    def pair_row(ref, k):
        return jnp.concatenate([ref[pl.ds(2 * k, 1), :], ref[pl.ds(2 * k + 1, 1), :]], axis=1)

    def mark(k, carry):
        row = pair_row(index, k)
        ids = lax.broadcasted_iota(jnp.int32, (6 * atoms, two), 0)
        onehot[k] = jnp.where(ids == row, 1.0, 0.0).astype(bf16)
        return carry

    lax.fori_loop(0, slots // 2, mark, 0)

    source_t = jnp.dot(mixed, wsrc_ref[...], preferred_element_type=f32).T
    source_t = source_t.astype(bf16).astype(f32)
    source[...] = jnp.concatenate([source_t, source_t], axis=1)
    wrad = wrad_ref[...]
    w_hi = wrad.astype(bf16)
    w_lo = (wrad - w_hi.astype(f32)).astype(bf16)
    split[...] = jnp.concatenate([w_hi, w_hi, w_lo], axis=0)
    centers = 1.0 + 5.0 * lax.broadcasted_iota(jnp.int32, (RADIAL, two), 0).astype(f32) / (
        RADIAL - 1
    )
    raw = lax.dot_general(
        wself_ref[...], mixed, (((0,), (1,)), ((), ())), preferred_element_type=f32
    )
    far[0:PAIRS, 0:atoms] = raw
    for i in range(ORBITALS):
        for j in range(i, ORBITALS):
            p, q = i * ORBITALS + j, j * ORBITALS + i
            mean = 0.5 * (far[p : p + 1, 0:atoms] + far[q : q + 1, 0:atoms])
            mean = mean.astype(bf16).astype(f32)
            blocks[slots, p : p + 1, :] = mean
            if p != q:
                blocks[slots, q : q + 1, :] = mean

    def block_apply(k, parts, acc):
        acc = list(acc)
        for j in range(ORBITALS):
            n = parts(j)
            for i in range(ORBITALS):
                acc[i] = acc[i] + blocks[k, pl.ds(i * ORBITALS + j, 1), :] * n
        return tuple(acc)

    def own_apply(vec, acc):
        return block_apply(slots, lambda j: vec[j * PROBES : (j + 1) * PROBES], acc)

    def gathered(k, acc, far):
        for h in range(2):
            acc = block_apply(
                2 * k + h,
                lambda j: far[
                    channels + j * PROBES : channels + (j + 1) * PROBES,
                    h * atoms : (h + 1) * atoms,
                ],
                acc,
            )
        return acc

    zero = tuple(jnp.zeros((PROBES, atoms), f32) for _ in range(ORBITALS))
    receive(0)

    def bond_make(k, far):
        length = pair_row(len_ref, k)
        basis = jnp.exp(-basis_sharpness * (length - centers) ** 2)
        b_hi = basis.astype(bf16)
        b_lo = (basis - b_hi.astype(f32)).astype(bf16)
        lifted = dot_tn(split[...], jnp.concatenate([b_hi, b_lo, b_hi], axis=0))
        edge = silu(source[...] + far[0:channels, :] + lifted).astype(bf16)
        hidden = silu(dot_tn(wmid_ref[...], edge)).astype(bf16)
        made = dot_tn(wout_ref[...], hidden) * pair_row(live_ref, k).astype(f32)
        made = made.astype(bf16).astype(f32)
        blocks[2 * k, 0:PAIRS, :] = made[:, 0:atoms]
        blocks[2 * k + 1, 0:PAIRS, :] = made[:, atoms:two]
        tall[0:PAIRS, :] += jnp.abs(made[:, 0:atoms]) + jnp.abs(made[:, atoms:two])

    def bond_step(m, acc):
        far[...] = jnp.dot(first[...], onehot[2 * m], preferred_element_type=f32)
        near[...] = jnp.dot(first[...], onehot[2 * m + 1], preferred_element_type=f32)
        bond_make(2 * m, far)
        bond_make(2 * m + 1, near)
        return gathered(2 * m + 1, gathered(2 * m, acc, far), near)

    tall[0:PAIRS, :] = jnp.abs(blocks[slots, 0:PAIRS, :])
    acc = lax.fori_loop(0, slots // 4, bond_step, own_apply(keep[0], zero))
    y1 = jnp.concatenate(acc, axis=0)
    vecs[0, :, own] = y1.astype(bf16)
    send(1)
    keep[1] = y1

    biggest = jnp.zeros((1, atoms), f32)
    for i in range(ORBITALS):
        row = jnp.sum(tall[i * ORBITALS : (i + 1) * ORBITALS, :], axis=0, keepdims=True)
        biggest = jnp.maximum(biggest, row)
    rad[0] = jnp.broadcast_to(biggest, rad.shape[1:])

    def radius_copy(q):
        return pltpu.make_async_remote_copy(
            src_ref=rad.at[q],
            dst_ref=rad.at[rounds + 1 + q],
            send_sem=rsend_sem.at[q],
            recv_sem=rrecv_sem.at[q],
            device_id=partner(q),
            device_id_type=MESH,
        )

    def radius_turn(q):
        radius_copy(q).wait_recv()
        rad[q + 1] = jnp.maximum(rad[q], rad[rounds + 1 + q])
        if q + 1 < rounds:
            radius_copy(q + 1).start()

    radius_copy(0).start()

    def gather(n, k, buf):
        buf[pl.ds(channels, VEC), :] = jnp.dot(vecs[n - 1], onehot[k], preferred_element_type=f32)

    def apply_part(n, lo, hi, acc):
        def step(m, acc):
            gather(n, 2 * m + 1, near)
            acc = gathered(2 * m, acc, far)
            gather(n, jnp.minimum(2 * m + 2, slots // 2 - 1), far)
            return gathered(2 * m + 1, acc, near)

        if lo == 0:
            gather(n, 0, far)
        return lax.fori_loop(lo, hi, step, acc)

    half = slots // 4
    acc = own_apply(y1, zero)
    radius_turn(0)
    radius_turn(1)
    receive(1)
    turns = list(range(2, rounds))
    cuts = [half * i // (len(turns) + 1) for i in range(len(turns) + 2)]
    for i in range(len(turns) + 1):
        acc = apply_part(1, cuts[i], cuts[i + 1], acc)
        if i < len(turns):
            radius_turn(turns[i])
    radius = jnp.max(rad[rounds], keepdims=True)
    scale = stretch_factor / radius

    t0 = keep[0]
    t1 = scale[0:1, 0:1] * keep[1]
    t2 = 2.0 * (scale[0:1, 0:1] * (scale[0:1, 0:1] * jnp.concatenate(acc, axis=0))) - t0
    vecs[1, :, own] = t2.astype(bf16)
    send(2)
    keep[1] = t1
    keep[2] = t2
    keep[0] = coef_ref[0] * t0 + coef_ref[1] * t1 + coef_ref[2] * t2
    acc = own_apply(keep[2], zero)
    receive(2)
    acc = apply_part(2, 0, half, acc)
    t3 = 2.0 * (scale[0:1, 0:1] * jnp.concatenate(acc, axis=0)) - keep[1]
    vecs[2, :, own] = t3.astype(bf16)
    send(3)
    keep[1] = t3
    keep[0] = keep[0] + coef_ref[3] * t3
    acc = own_apply(keep[1], zero)
    receive(3)
    acc = apply_part(3, 0, half, acc)
    t4 = 2.0 * (scale[0:1, 0:1] * jnp.concatenate(acc, axis=0)) - keep[2]
    tall[0:VEC, :] = keep[0] + coef_ref[4] * t4
    tall[VEC:, :] = jnp.zeros((tall.shape[0] - VEC, atoms), f32)
    for i in range(tall.shape[0] // atoms):
        wide[:, i * atoms : (i + 1) * atoms] = tall[i * atoms : (i + 1) * atoms, :].T
    out_ref[...] = wide[:, 0:VEC]
    for n in range(STEPS):
        finish(n)
    for q in range(rounds):
        radius_copy(q).wait_send()


def body(n_rows, *args):
    (node, species, embed, wsrc, wdst, wrad, wmid, wout, wself, tgt, live, length, probes, coef) = args
    atoms = node.shape[2]
    slots = tgt.shape[2]
    channels = wsrc.shape[1]
    rounds = n_rows.bit_length()
    vmem = pl.BlockSpec(memory_space=pltpu.VMEM)
    lanes = 2 * atoms
    tall_rows = 2 * atoms
    out = pl.pallas_call(
        functools.partial(kernel, n_rows, rounds),
        out_shape=jax.ShapeDtypeStruct((atoms, VEC), f32),
        in_specs=[vmem] * 13 + [pl.BlockSpec(memory_space=pltpu.SMEM)],
        out_specs=vmem,
        scratch_shapes=[
            pltpu.VMEM((channels + VEC, 6 * atoms), bf16),
            pltpu.VMEM((STEPS - 1, VEC, 6 * atoms), bf16),
            pltpu.VMEM((slots // 2, 6 * atoms, lanes), bf16),
            pltpu.VMEM((slots, atoms), jnp.int32),
            pltpu.VMEM((slots + 1, SPAN, atoms), f32),
            pltpu.VMEM((channels, lanes), f32),
            pltpu.VMEM((3 * RADIAL, channels), bf16),
            pltpu.VMEM((3, VEC, atoms), f32),
            pltpu.VMEM((atoms, tall_rows), f32),
            pltpu.VMEM((tall_rows, atoms), f32),
            pltpu.VMEM((2 * rounds + 1, 8, atoms), f32),
            pltpu.VMEM((channels + VEC, lanes), f32),
            pltpu.VMEM((channels + VEC, lanes), f32),
            pltpu.SemaphoreType.DMA((STEPS, 5)),
            pltpu.SemaphoreType.DMA((STEPS, 5)),
            pltpu.SemaphoreType.DMA((rounds,)),
            pltpu.SemaphoreType.DMA((rounds,)),
        ],
        compiler_params=pltpu.CompilerParams(
            collective_id=0, has_side_effects=True, vmem_limit_bytes=40 * 1024 * 1024
        ),
    )(
        node[0, 0], species[0], embed, wsrc, wdst, wrad, wmid, wout, wself,
        tgt[0, 0], live[0, 0], length[0, 0], probes[0, 0], coef,
    )
    return out[None, None]


def solution(mesh):
    n_rows = mesh.shape["rows"]
    block4 = P("rows", "cols", None, None)
    placed = (
        block4, P("rows", "cols", None), P(), P(), P(), P(), P(), P(), P(),
        block4, block4, block4, block4, P(),
    )
    return jax.shard_map(
        functools.partial(body, n_rows), mesh=mesh, in_specs=placed, out_specs=block4, check_vma=False
    )
```
